512 devices in a mesh: row: 16 (over y, x_hi), col: 8 (over z), depth: 4 (over x_lo, core).
Axes of the slice: x: 4 (x_hi: 2, x_lo: 2; x = x_hi * 2 + x_lo), y: 8, z: 8, core: 2. Of those that a mesh axis runs over, the one named last changes fastest.
Arguments:
- slab_parts: float32 [4, 32768, 2048], P('depth', 'row', 'col'), may hold values from -6 to 6
- panel_t: float32 [256, 32768], P('col', 'row'), may hold values from -6 to 6
- l_inv: float32 [256, 256], replicated, as said below
- u_inv: float32 [256, 256], replicated, as said below
- pivots: int32 [256], replicated, may hold values from 0 to 32767, as said below
Outputs:
- updated: float32 [32768, 2048], P(('row', 'depth'), 'col')
The draws below stay inside these ranges and needn't reach their ends.
Inputs may be any that keep to these rules, and one draw needn't show every extreme that they name: `pivots`: entry i lies between i and 32767; entry 0 is 0. `l_inv`: unit lower triangular. `u_inv`: upper triangular with a positive diagonal.
All inputs are finite; a program needn't handle non-finite values.
Results may differ from the reference program's by a relative error of at most 0.00007.
Values sent between devices are 32-bit elements; how exact they have to be, the bound alone decides.
No kernel may reach another device: no remote copies, remote signals or barrier semaphores. Data moves between devices by JAX's collectives and lax.ppermute only.
A program may use at most 64 MiB of HBM per device.

```python
import jax
import jax.numpy as jnp
from jax import lax

MR_DEV = 2048
PANEL = 256
SLAB = 2048
M = 32768
N_ROW = 16
N_DEPTH = 4


def draw_l_inv(key, part):
    key = jax.random.fold_in(key, 2)
    values = jax.random.normal(key, (PANEL, PANEL), jnp.float32) * (0.5 / PANEL ** 0.5)
    return jnp.tril(values, -1) + jnp.eye(PANEL, dtype=jnp.float32)


def draw_u_inv(key, part):
    key = jax.random.fold_in(key, 3)
    first_key, second_key = jax.random.split(key)
    values = jax.random.normal(first_key, (PANEL, PANEL), jnp.float32) * (0.15 / PANEL ** 0.5)
    logs = jax.random.uniform(second_key, (PANEL,), jnp.float32, jnp.log(0.06), jnp.log(0.25))
    return jnp.triu(values, 1) + jnp.diag(jnp.exp(logs))


def draw_pivots(key, part):
    key = jax.random.fold_in(key, 5)
    keys = jax.random.split(key, 5)
    steps = jnp.arange(PANEL, dtype=jnp.int32)
    hot_device = jax.random.randint(keys[0], (), 0, N_ROW)
    spread = jax.random.randint(keys[1], (PANEL,), steps, M)
    near_hot = hot_device * MR_DEV + jax.random.randint(keys[2], (PANEL,), 0, MR_DEV)
    coins = jax.random.randint(keys[3], (PANEL,), 0, 2)
    chosen = jnp.where(coins == 1, jnp.maximum(near_hot, steps), spread)
    last_slot = jax.random.randint(keys[4], (), 1, PANEL)
    chosen = chosen.at[0].set(0)
    return chosen.at[last_slot].set(M - 1).astype(jnp.int32)


def shard_levels(rng, shape, cuts, smallest, largest):
    loudness = 1.0
    for position, blocks in cuts:
        draws = jax.random.uniform(jax.random.fold_in(jax.random.fold_in(rng, 6), position), (blocks,), jnp.float32, smallest / len(cuts), largest / len(cuts))
        loudness = loudness * jnp.repeat(jnp.exp(draws), shape[position] // blocks).reshape((-1,) + (1,) * (len(shape) - 1 - position))
    return loudness


def scatter_about(rng, shape, width, bound, shards=(), held_as=jnp.bfloat16):
    result = jax.random.normal(rng, shape, jnp.float32) * width
    if len(shards) > 0:
        result = shard_levels(rng, shape, shards, -0.22, 0.18) * result
    return jnp.clip(result, min=-bound, max=bound).astype(held_as)


def setup_inputs(seed: int = 0) -> dict:
    seeds = jax.random.split(jax.random.key(seed), 6)
    slab_parts = scatter_about(seeds[0], (N_DEPTH, M, SLAB), 1.0, 6.0, ((0, 4), (1, 16), (2, 8)), jnp.float32)
    panel_t = scatter_about(seeds[1], (PANEL, M), 1.0, 6.0, ((0, 8), (1, 16)), jnp.float32)
    l_inv = draw_l_inv(jax.random.fold_in(seeds[5], 71), 0)
    u_inv = draw_u_inv(jax.random.fold_in(seeds[5], 71), 0)
    pivots = draw_pivots(jax.random.fold_in(seeds[5], 71), 0)
    return dict(slab_parts=slab_parts, panel_t=panel_t, l_inv=l_inv, u_inv=u_inv, pivots=pivots)


def pivot_order(pivots, count):
    def swap_one(i, row_order):
        j = pivots[i]
        first_val = row_order[i]
        second_val = row_order[j]
        return row_order.at[i].set(second_val).at[j].set(first_val)
    start_order = jnp.arange(count, dtype=jnp.int32)
    return lax.fori_loop(0, pivots.shape[0], swap_one, start_order)


def reference(slab_parts, panel_t, l_inv, u_inv, pivots):
    highest = lax.Precision.HIGHEST
    slab_block = jnp.sum(slab_parts, axis=0)
    row_order = pivot_order(pivots, M)
    slab_p = slab_block[row_order]
    panel_p = panel_t[:, row_order]
    lower = lax.dot_general(panel_p, u_inv, (((0,), (0,)), ((), ())), precision=highest, preferred_element_type=jnp.float32)
    upper = jnp.dot(l_inv, slab_p[:PANEL], precision=highest, preferred_element_type=jnp.float32)
    remain = slab_p - jnp.dot(lower, upper, precision=highest, preferred_element_type=jnp.float32)
    return jnp.concatenate([upper, remain[PANEL:]], axis=0)
```

```python
import functools

import jax
import jax.numpy as jnp
from jax import lax
from jax.experimental import pallas as pl
from jax.experimental.pallas import tpu as pltpu
from jax.sharding import Mesh
from jax.sharding import PartitionSpec as P

ROW = ("y", "xh")
DEPTH = ("xl", "core")
PLANE = ("xh", "xl", "core")
HIGHEST = lax.Precision.HIGHEST
F32 = jnp.float32
I32 = jnp.int32
VMEM = pl.BlockSpec(memory_space=pltpu.VMEM)
SMEM = pl.BlockSpec(memory_space=pltpu.SMEM)
ANY = pl.BlockSpec(memory_space=pl.ANY)


def lane_lookup(table, index):
    width = table.shape[1]
    parts = []
    for at in range(0, width, 128):
        wanted = index[:, at : at + 128]
        found = jnp.zeros_like(wanted)
        for start in range(0, width, 128):
            chunk = table[:, start : start + 128]
            taken = jnp.take_along_axis(chunk, wanted & 127, axis=1)
            found = jnp.where((wanted >= start) & (wanted < start + 128), taken, found)
        parts.append(found)
    return jnp.concatenate(parts, axis=1)


def pivot_kernel(place, pivots, slab_hbm, send, top_row, top_col, slab, source_v, source_s, sems):
    rows, columns = slab.shape
    width = pivots.shape[1]
    groups, both, _ = send.shape
    block = both // 2
    share = top_row.shape[1]
    row_start = place[0]
    share_start = place[1]
    fetch = pltpu.make_async_copy(slab_hbm, slab, sems.at[0])
    fetch.start()
    along = lax.broadcasted_iota(I32, (width, width), 1)
    down = lax.broadcasted_iota(I32, (width, width), 0)
    pivot_row = pivots[...]
    pivot_all = jnp.broadcast_to(pivot_row, (width, width))
    pivot_col = jnp.max(jnp.where(along == down, pivot_all, -1), axis=1, keepdims=True)
    earlier = down < along
    same = pivot_col == pivot_all
    before = jnp.max(jnp.where((pivot_col == along) & earlier, down, -1), axis=0, keepdims=True)
    last = jnp.max(jnp.where(same & earlier, down, -1), axis=0, keepdims=True)
    later = jnp.max(jnp.where(same & (down > along), 1, 0), axis=0, keepdims=True)
    slots = lax.broadcasted_iota(I32, (8, width), 1)
    before = jnp.broadcast_to(before, (8, width))
    content = jnp.where(before < 0, slots, before)
    span = 1
    while span < width:
        content = lane_lookup(content, content)
        span *= 2
    last = jnp.broadcast_to(last, (8, width))
    source = jnp.where(
        last < 0,
        jnp.broadcast_to(pivot_row, (8, width)),
        lane_lookup(content, jnp.maximum(last, 0)),
    )
    source_v[...] = source
    to_scalar = pltpu.make_async_copy(source_v, source_s, sems.at[1])
    to_scalar.start()
    content_row = content[:1]
    target_row = jnp.where((later == 0) & (pivot_row >= width), pivot_row, -1)
    content_col = jnp.max(
        jnp.where(along == down, jnp.broadcast_to(content_row, (width, width)), -1),
        axis=1,
        keepdims=True,
    )
    target_col = jnp.max(
        jnp.where(along == down, jnp.broadcast_to(target_row, (width, width)), -1),
        axis=1,
        keepdims=True,
    )
    own_along = share_start + lax.broadcasted_iota(I32, (width, share), 1)
    top_row[...] = jnp.max(jnp.where(target_col == own_along, content_col, -1), axis=0, keepdims=True)
    own_down = share_start + lax.broadcasted_iota(I32, (share, width), 0)
    found = jnp.max(jnp.where(target_row == own_down, content_row, -1), axis=1, keepdims=True)
    top_col[...] = jnp.broadcast_to(found, top_col.shape)
    fetch.wait()
    for group in range(groups):
        send[group, block:, :] = slab[group * block : (group + 1) * block, :]
    to_scalar.wait()

    def gather(group, carry):
        for slot in range(block):
            local = source_s[0, group * block + slot] - row_start
            owned = (local >= 0) & (local < rows)
            at = jnp.where(owned, local, 0)
            keep = jnp.where(owned, 1.0, 0.0).astype(F32)
            send[group, slot : slot + 1, :] = slab[pl.ds(at, 1), :] * keep
        return carry

    lax.fori_loop(0, groups, gather, 0)


def plane_sum_kernel(got, send):
    groups, both, _ = got.shape
    block = both // 2
    first = groups // 2
    moved = got[0, :block, :]
    for source in range(1, groups):
        moved = moved + got[source, :block, :]
    top = got[0, block:, :]
    for source in range(1, first):
        top = top + got[source, block:, :]
    for target in range(send.shape[0]):
        send[target, :block, :] = moved
        send[target, block:, :] = top


def column_kernel(place, got, panel, top_panel, top_row, rows_out, panel_out):
    groups, both, _ = got.shape
    block = both // 2
    moved = got[0, :block, :]
    for source in range(1, groups):
        moved = moved + got[source, :block, :]
    rows_out[:block, :] = moved
    rows_out[block:, :] = got[0, block:, :]
    share = top_row.shape[1]
    width = top_panel.shape[1]
    lands = top_row[...]
    slot = lax.broadcasted_iota(I32, (width, share), 0)
    chosen = jnp.where(slot == lands, 1.0, 0.0).astype(F32)
    replaced = jnp.dot(top_panel[...], chosen, precision=HIGHEST, preferred_element_type=F32)
    own = panel[:, pl.ds(pl.multiple_of(place[2] * share, share), share)]
    fixed = jnp.where(lands >= 0, replaced, own)
    for target in range(panel_out.shape[0]):
        panel_out[target] = fixed


def update_kernel(place, slab, panel, rows_in, l_inv, u_inv, top_col, out):
    groups, both, columns = rows_in.shape
    block = both // 2
    width = l_inv.shape[0]
    share = slab.shape[0]
    panel_p = panel[...].reshape(width, share)
    lower = lax.dot_general(
        panel_p, u_inv[...], (((0,), (0,)), ((), ())), precision=HIGHEST, preferred_element_type=F32
    )
    moved = rows_in[:, :block, :].reshape(width, columns)
    top = rows_in[:, block:, :].reshape(width, columns)
    upper = jnp.dot(l_inv[...], moved, precision=HIGHEST, preferred_element_type=F32)
    lands = top_col[:, :1]
    slot = lax.broadcasted_iota(I32, (share, width), 1)
    chosen = jnp.where(slot == lands, 1.0, 0.0).astype(F32)
    replaced = jnp.dot(chosen, top, precision=HIGHEST, preferred_element_type=F32)
    slab_p = jnp.where(lands >= 0, replaced, slab[...])
    out[...] = slab_p - jnp.dot(lower, upper, precision=HIGHEST, preferred_element_type=F32)

    @pl.when(place[1] == 0)
    def _():
        out[:width, :] = upper


def shards(slab_parts, panel_t, l_inv, u_inv, pivots):
    slab_local = slab_parts[0]
    rows, columns = slab_local.shape
    width = l_inv.shape[0]
    tall = panel_t.shape[0]
    n_y, n_z = lax.axis_size("y"), lax.axis_size("z")
    n_depth = lax.axis_size(DEPTH)
    n_plane = lax.axis_size(PLANE)
    share = rows // n_depth
    block = width // n_plane
    row_index = lax.axis_index(ROW)
    layer = lax.axis_index(DEPTH)
    row_start = row_index * rows
    place = jnp.stack([row_start, row_start + layer * share, layer]).astype(I32)

    slab_sum = lax.psum_scatter(slab_local, DEPTH, scatter_dimension=0, tiled=True)

    send, top_row, top_col = pl.pallas_call(
        pivot_kernel,
        out_shape=(
            jax.ShapeDtypeStruct((n_plane, 2 * block, columns), F32),
            jax.ShapeDtypeStruct((1, share), I32),
            jax.ShapeDtypeStruct((share, 128), I32),
        ),
        in_specs=[SMEM, VMEM, ANY],
        out_specs=(VMEM, VMEM, VMEM),
        scratch_shapes=[
            pltpu.VMEM((rows, columns), F32),
            pltpu.VMEM((8, width), I32),
            pltpu.SMEM((8, width), I32),
            pltpu.SemaphoreType.DMA((2,)),
        ],
        compiler_params=pltpu.CompilerParams(vmem_limit_bytes=32 << 20),
        name="pivot_rows",
    )(place, pivots.reshape(1, width), slab_local)

    top_panel = jnp.where(row_index == 0, panel_t[:, :width], 0.0)
    step = n_y // 2
    while step >= 1:
        pairs = [(at, at + step) for at in range(0, n_y, 2 * step)]
        top_panel = top_panel + lax.ppermute(top_panel, "y", pairs)
        step //= 2
    top_panel = top_panel + lax.ppermute(top_panel, "xh", [(0, 1)])

    got = lax.all_to_all(send, PLANE, 0, 0)
    send = pl.pallas_call(
        plane_sum_kernel,
        out_shape=jax.ShapeDtypeStruct((n_y, 2 * block, columns), F32),
        in_specs=[VMEM],
        out_specs=VMEM,
        compiler_params=pltpu.CompilerParams(vmem_limit_bytes=32 << 20),
        name="plane_sum",
    )(got)
    got = lax.all_to_all(send, "y", 0, 0)
    rows_out, panel_out = pl.pallas_call(
        column_kernel,
        out_shape=(
            jax.ShapeDtypeStruct((2 * block, columns), F32),
            jax.ShapeDtypeStruct((n_z, tall, share), F32),
        ),
        in_specs=[SMEM, VMEM, VMEM, VMEM, VMEM],
        out_specs=(VMEM, VMEM),
        compiler_params=pltpu.CompilerParams(vmem_limit_bytes=32 << 20),
        name="column_sum",
    )(place, got, panel_t, top_panel, top_row)
    panel_p = lax.all_to_all(panel_out, "z", 0, 0)
    rows_in = lax.all_gather(rows_out, PLANE)
    return pl.pallas_call(
        update_kernel,
        out_shape=jax.ShapeDtypeStruct((share, columns), F32),
        in_specs=[SMEM, VMEM, VMEM, VMEM, VMEM, VMEM, VMEM],
        out_specs=VMEM,
        compiler_params=pltpu.CompilerParams(vmem_limit_bytes=32 << 20),
        name="update_rows",
    )(place, slab_sum, panel_p, rows_in, l_inv, u_inv, top_col)


def solution(mesh):
    n_row, n_col, n_depth = mesh.devices.shape
    fine = Mesh(
        mesh.devices.reshape(n_row // 2, 2, n_col, n_depth // 2, 2), ("y", "xh", "z", "xl", "core")
    )
    placed = (P(DEPTH, ROW, "z"), P("z", ROW), P(), P(), P())
    return jax.shard_map(
        shards,
        mesh=fine,
        in_specs=placed,
        out_specs=P(("y", "xh", "xl", "core"), "z"),
        check_vma=False,
    )
```

```python
import functools

import jax
import jax.numpy as jnp
from jax import lax
from jax.experimental import pallas as pl
from jax.experimental.pallas import tpu as pltpu
from jax.sharding import Mesh
from jax.sharding import PartitionSpec as P

ROW = ("y", "xh")
DEPTH = ("xl", "core")
PLANE = ("xh", "xl", "core")
HIGHEST = lax.Precision.HIGHEST
F32 = jnp.float32
I32 = jnp.int32
ANY = pl.BlockSpec(memory_space=pl.ANY)
VMEM = pl.BlockSpec(memory_space=pltpu.VMEM)
SMEM = pl.BlockSpec(memory_space=pltpu.SMEM)


def lane_lookup(table, index):
    width = table.shape[1]
    parts = []
    for at in range(0, width, 128):
        wanted = index[:, at : at + 128]
        found = jnp.zeros_like(wanted)
        for start in range(0, width, 128):
            chunk = table[:, start : start + 128]
            taken = jnp.take_along_axis(chunk, wanted & 127, axis=1)
            found = jnp.where((wanted >= start) & (wanted < start + 128), taken, found)
        parts.append(found)
    return jnp.concatenate(parts, axis=1)


def top_kernel(slab, panel, send, sems, *, layers):
    groups, both, _ = send.shape
    fill = panel.shape[0] // layers
    block = both - fill
    width = groups * block
    start = pl.multiple_of(lax.axis_index(DEPTH) * fill, fill)
    copies = []
    for target in range(groups):
        rows = slab.at[pl.ds(target * block, block), :]
        part = panel.at[pl.ds(start, fill), pl.ds(0, width)]
        copies.append(pltpu.make_async_copy(rows, send.at[target, pl.ds(0, block)], sems.at[0, target]))
        copies.append(pltpu.make_async_copy(part, send.at[target, pl.ds(block, fill)], sems.at[1, target]))
    for copy in copies:
        copy.start()
    for copy in copies:
        copy.wait()


def pivot_kernel(place, pivots, slab, send, top_row, top_col, give, source_v, source_s, sem):
    rows, columns = slab.shape
    width = pivots.shape[1]
    groups, block, _ = send.shape
    share = top_row.shape[1]
    row_start = place[0]
    share_start = place[1]
    along = lax.broadcasted_iota(I32, (width, width), 1)
    down = lax.broadcasted_iota(I32, (width, width), 0)
    pivot_row = pivots[...]
    pivot_all = jnp.broadcast_to(pivot_row, (width, width))
    pivot_col = jnp.max(jnp.where(along == down, pivot_all, -1), axis=1, keepdims=True)
    earlier = down < along
    same = pivot_col == pivot_all
    before = jnp.max(jnp.where((pivot_col == along) & earlier, down, -1), axis=0, keepdims=True)
    last = jnp.max(jnp.where(same & earlier, down, -1), axis=0, keepdims=True)
    later = jnp.max(jnp.where(same & (down > along), 1, 0), axis=0, keepdims=True)
    slots = lax.broadcasted_iota(I32, (8, width), 1)
    before = jnp.broadcast_to(before, (8, width))
    content = jnp.where(before < 0, slots, before)
    span = 1
    while span < width:
        content = lane_lookup(content, content)
        span *= 2
    last = jnp.broadcast_to(last, (8, width))
    source = jnp.where(
        last < 0,
        jnp.broadcast_to(pivot_row, (8, width)),
        lane_lookup(content, jnp.maximum(last, 0)),
    )
    source_v[...] = source
    to_scalar = pltpu.make_async_copy(source_v, source_s, sem)
    to_scalar.start()
    content_row = content[:1]
    target_row = jnp.where((later == 0) & (pivot_row >= width), pivot_row, -1)
    content_col = jnp.max(
        jnp.where(along == down, jnp.broadcast_to(content_row, (width, width)), -1),
        axis=1,
        keepdims=True,
    )
    target_col = jnp.max(
        jnp.where(along == down, jnp.broadcast_to(target_row, (width, width)), -1),
        axis=1,
        keepdims=True,
    )
    own_along = share_start + lax.broadcasted_iota(I32, (width, share), 1)
    top_row[...] = jnp.max(jnp.where(target_col == own_along, content_col, -1), axis=0, keepdims=True)
    own_down = share_start + lax.broadcasted_iota(I32, (share, width), 0)
    found = jnp.max(jnp.where(target_row == own_down, content_row, -1), axis=1, keepdims=True)
    top_col[...] = jnp.broadcast_to(found, top_col.shape)
    for half in range(give.shape[0]):
        start = pl.multiple_of((2 * half + place[3]) * share, share)
        give[half] = slab[pl.ds(start, share), :]
    to_scalar.wait()

    def gather(group, carry):
        for slot in range(block):
            local = source_s[0, group * block + slot] - row_start
            owned = (local >= 0) & (local < rows)
            at = jnp.where(owned, local, 0)
            keep = jnp.where(owned, 1.0, 0.0).astype(F32)
            send[group, slot : slot + 1, :] = slab[pl.ds(at, 1), :] * keep
        return carry

    lax.fori_loop(0, groups, gather, 0)


def pack_kernel(moved, got, send):
    groups, block, _ = moved.shape
    part = send.shape[1] - got.shape[1]
    for target in range(groups):
        send[target, :block, :] = moved[target]
    fill = got.shape[1] - block
    for target in range(groups):
        send[target, block : block + fill, :] = got[0, block:, :]
        send[target, block + fill :, :] = got[0, target * part : (target + 1) * part, :]


def plane_sum_kernel(place, got, panel, top_row, send, panel_out, top_panel, *, block):
    groups = got.shape[0]
    first = groups // 2
    part = send.shape[1] - block
    fill = got.shape[1] - block - part
    moved = got[0, :block, :]
    for source in range(1, groups):
        moved = moved + got[source, :block, :]
    top = got[0, block + fill :, :]
    for source in range(1, first):
        top = top + got[source, block + fill :, :]
    for target in range(send.shape[0]):
        send[target, :block, :] = moved
        send[target, block:, :] = top
    for source in range(first):
        top_panel[source * fill : (source + 1) * fill, :] = got[source, block : block + fill, :]
    share = top_row.shape[1]
    width = top_panel.shape[1]
    lands = top_row[...]
    slot = lax.broadcasted_iota(I32, (width, share), 0)
    chosen = jnp.where(slot == lands, 1.0, 0.0).astype(F32)
    replaced = jnp.dot(top_panel[...], chosen, precision=HIGHEST, preferred_element_type=F32)
    own = panel[:, pl.ds(pl.multiple_of(place[2] * share, share), share)]
    panel_out[...] = jnp.where(lands >= 0, replaced, own)


def column_kernel(got, panel, rows_out, panel_out):
    groups, both, _ = got.shape
    block = rows_out.shape[0] // 2
    part = both - block
    moved = got[0, :block, :]
    for source in range(1, groups):
        moved = moved + got[source, :block, :]
    rows_out[:block, :] = moved
    for source in range(groups):
        rows_out[block + source * part : block + (source + 1) * part, :] = got[source, block:, :]
    for target in range(panel_out.shape[0]):
        panel_out[target] = panel[...]


def update_kernel(place, slab, slab_got, panel, rows_in, l_inv, u_inv, top_col, out, *, n_y):
    groups, both, columns = rows_in.shape
    block = both // 2
    part = block // n_y
    width = l_inv.shape[0]
    share = slab.shape[0]
    panel_p = panel[...].reshape(width, share)
    lower = lax.dot_general(
        panel_p, u_inv[...], (((0,), (0,)), ((), ())), precision=HIGHEST, preferred_element_type=F32
    )
    moved = rows_in[:, :block, :].reshape(width, columns)
    top = rows_in[:, block:, :].reshape(width, columns)
    upper = jnp.dot(l_inv[...], moved, precision=HIGHEST, preferred_element_type=F32)
    lands = top_col[:, :1]
    slot = lax.broadcasted_iota(I32, (share, width), 1)
    member, rest = slot // block, slot % block
    holds = (rest // part) * (groups * part) + member * part + rest % part
    chosen = jnp.where(holds == lands, 1.0, 0.0).astype(F32)
    replaced = jnp.dot(chosen, top, precision=HIGHEST, preferred_element_type=F32)
    slab_p = jnp.where(lands >= 0, replaced, slab[...] + slab_got[...])
    out[...] = slab_p - jnp.dot(lower, upper, precision=HIGHEST, preferred_element_type=F32)

    @pl.when(place[1] == 0)
    def _():
        out[:width, :] = upper


def shards(slab_parts, panel_t, l_inv, u_inv, pivots):
    slab_local = slab_parts[0]
    rows, columns = slab_local.shape
    width = l_inv.shape[0]
    tall = panel_t.shape[0]
    n_y, n_z = lax.axis_size("y"), lax.axis_size("z")
    n_depth = lax.axis_size(DEPTH)
    n_plane = lax.axis_size(PLANE)
    share = rows // n_depth
    block = width // n_plane
    part = block // n_y
    fill = tall // n_depth
    row_index = lax.axis_index(ROW)
    layer = lax.axis_index(DEPTH)
    x_index = lax.axis_index("xl")
    core = lax.axis_index("core")
    row_start = row_index * rows
    place = jnp.stack([row_start, row_start + layer * share, layer, 1 - core]).astype(I32)
    swap = [(0, 1), (1, 0)]
    params = pltpu.CompilerParams(vmem_limit_bytes=32 << 20)

    wide = pltpu.CompilerParams(vmem_limit_bytes=56 << 20)

    top = pl.pallas_call(
        functools.partial(top_kernel, layers=n_depth),
        out_shape=jax.ShapeDtypeStruct((n_y, width // n_y + fill, columns), F32),
        in_specs=[ANY, ANY],
        out_specs=VMEM,
        scratch_shapes=[pltpu.SemaphoreType.DMA((2, n_y))],
        compiler_params=wide,
        name="top_rows",
    )(slab_local, panel_t)
    top, place = lax.optimization_barrier((top, place))
    top = lax.all_to_all(top, "y", 0, 0)

    moved, top_row, top_col, give = pl.pallas_call(
        pivot_kernel,
        out_shape=(
            jax.ShapeDtypeStruct((n_plane, block, columns), F32),
            jax.ShapeDtypeStruct((1, share), I32),
            jax.ShapeDtypeStruct((share, 128), I32),
            jax.ShapeDtypeStruct((n_depth // 2, share, columns), F32),
        ),
        in_specs=[SMEM, VMEM, VMEM],
        out_specs=(VMEM, VMEM, VMEM, VMEM),
        scratch_shapes=[
            pltpu.VMEM((8, width), I32),
            pltpu.SMEM((8, width), I32),
            pltpu.SemaphoreType.DMA,
        ],
        compiler_params=params,
        cost_estimate=pl.CostEstimate(
            flops=2 * width * rows * columns, bytes_accessed=16 * rows * columns, transcendentals=0
        ),
        name="pivot_rows",
    )(place, pivots.reshape(1, width), slab_local)

    send = pl.pallas_call(
        pack_kernel,
        out_shape=jax.ShapeDtypeStruct((n_plane, block + fill + part, columns), F32),
        in_specs=[VMEM, VMEM],
        out_specs=VMEM,
        compiler_params=params,
        name="pack_plane",
    )(moved, top)
    send, give = lax.optimization_barrier((send, give))
    core_got = lax.ppermute(give, "core", swap)
    by_core = slab_local.reshape(n_depth // 2, 2, share, columns)
    half = lax.dynamic_index_in_dim(by_core, core, 1, keepdims=False) + core_got
    slab_own = lax.dynamic_index_in_dim(half, x_index, 0, keepdims=False)
    slab_give = lax.dynamic_index_in_dim(half, 1 - x_index, 0, keepdims=False)
    got = lax.all_to_all(send, PLANE, 0, 0)
    send, panel_own = pl.pallas_call(
        functools.partial(plane_sum_kernel, block=block),
        out_shape=(
            jax.ShapeDtypeStruct((n_y, block + part, columns), F32),
            jax.ShapeDtypeStruct((tall, share), F32),
        ),
        in_specs=[SMEM, VMEM, VMEM, VMEM],
        out_specs=(VMEM, VMEM),
        scratch_shapes=[pltpu.VMEM((tall, width), F32)],
        compiler_params=params,
        name="plane_sum",
    )(place, got, panel_t, top_row)
    send, slab_own, slab_give = lax.optimization_barrier((send, slab_own, slab_give))
    slab_got = lax.ppermute(slab_give, "xl", swap)
    got = lax.all_to_all(send, "y", 0, 0)
    got, slab_got = lax.optimization_barrier((got, slab_got))
    rows_out, panel_out = pl.pallas_call(
        column_kernel,
        out_shape=(
            jax.ShapeDtypeStruct((2 * block, columns), F32),
            jax.ShapeDtypeStruct((n_z, tall, share), F32),
        ),
        in_specs=[VMEM, VMEM],
        out_specs=(VMEM, VMEM),
        compiler_params=params,
        name="column_sum",
    )(got, panel_own)
    panel_p = lax.all_to_all(panel_out, "z", 0, 0)
    rows_in = lax.all_gather(rows_out, PLANE)
    return pl.pallas_call(
        functools.partial(update_kernel, n_y=n_y),
        out_shape=jax.ShapeDtypeStruct((share, columns), F32),
        in_specs=[SMEM] + [VMEM] * 7,
        out_specs=VMEM,
        compiler_params=params,
        name="update_rows",
    )(place, slab_own, slab_got, panel_p, rows_in, l_inv, u_inv, top_col)


def solution(mesh):
    n_row, n_col, n_depth = mesh.devices.shape
    fine = Mesh(
        mesh.devices.reshape(n_row // 2, 2, n_col, n_depth // 2, 2), ("y", "xh", "z", "xl", "core")
    )
    placed = (P(DEPTH, ROW, "z"), P("z", ROW), P(), P(), P())
    return jax.shard_map(
        shards,
        mesh=fine,
        in_specs=placed,
        out_specs=P(("y", "xh", "xl", "core"), "z"),
        check_vma=False,
    )
```

```python
import functools

import jax
import jax.numpy as jnp
from jax import lax
from jax.experimental import pallas as pl
from jax.experimental.pallas import tpu as pltpu
from jax.sharding import Mesh
from jax.sharding import PartitionSpec as P

ROW = ("y", "xh")
DEPTH = ("xl", "core")
PLANE = ("xh", "xl", "core")
HIGHEST = lax.Precision.HIGHEST
F32 = jnp.float32
I32 = jnp.int32
ANY = pl.BlockSpec(memory_space=pl.ANY)
VMEM = pl.BlockSpec(memory_space=pltpu.VMEM)
SMEM = pl.BlockSpec(memory_space=pltpu.SMEM)


def lane_lookup(table, index):
    width = table.shape[1]
    parts = []
    for at in range(0, width, 128):
        wanted = index[:, at : at + 128]
        found = jnp.zeros_like(wanted)
        for start in range(0, width, 128):
            chunk = table[:, start : start + 128]
            taken = jnp.take_along_axis(chunk, wanted & 127, axis=1)
            found = jnp.where((wanted >= start) & (wanted < start + 128), taken, found)
        parts.append(found)
    return jnp.concatenate(parts, axis=1)


def top_kernel(slab, panel, send, sems, *, layers):
    groups, both, _ = send.shape
    fill = panel.shape[0] // layers
    block = both - fill
    width = groups * block
    start = pl.multiple_of(lax.axis_index(DEPTH) * fill, fill)
    copies = []
    for target in range(groups):
        rows = slab.at[pl.ds(target * block, block), :]
        part = panel.at[pl.ds(start, fill), pl.ds(0, width)]
        copies.append(pltpu.make_async_copy(rows, send.at[target, pl.ds(0, block)], sems.at[0, target]))
        copies.append(pltpu.make_async_copy(part, send.at[target, pl.ds(block, fill)], sems.at[1, target]))
    for copy in copies:
        copy.start()
    for copy in copies:
        copy.wait()


def pivot_kernel(place, pivots, slab, send, top_row, top_col, give, source_v, source_s, sem):
    rows, columns = slab.shape
    width = pivots.shape[1]
    groups, block, _ = send.shape
    share = top_row.shape[1]
    row_start = place[0]
    share_start = place[1]
    along = lax.broadcasted_iota(I32, (width, width), 1)
    down = lax.broadcasted_iota(I32, (width, width), 0)
    pivot_row = pivots[...]
    pivot_all = jnp.broadcast_to(pivot_row, (width, width))
    pivot_col = jnp.max(jnp.where(along == down, pivot_all, -1), axis=1, keepdims=True)
    earlier = down < along
    same = pivot_col == pivot_all
    before = jnp.max(jnp.where((pivot_col == along) & earlier, down, -1), axis=0, keepdims=True)
    last = jnp.max(jnp.where(same & earlier, down, -1), axis=0, keepdims=True)
    later = jnp.max(jnp.where(same & (down > along), 1, 0), axis=0, keepdims=True)
    slots = lax.broadcasted_iota(I32, (8, width), 1)
    before = jnp.broadcast_to(before, (8, width))
    content = jnp.where(before < 0, slots, before)
    span = 1
    while span < width:
        content = lane_lookup(content, content)
        span *= 2
    last = jnp.broadcast_to(last, (8, width))
    source = jnp.where(
        last < 0,
        jnp.broadcast_to(pivot_row, (8, width)),
        lane_lookup(content, jnp.maximum(last, 0)),
    )
    source_v[...] = source
    to_scalar = pltpu.make_async_copy(source_v, source_s, sem)
    to_scalar.start()
    content_row = content[:1]
    target_row = jnp.where((later == 0) & (pivot_row >= width), pivot_row, -1)
    content_col = jnp.max(
        jnp.where(along == down, jnp.broadcast_to(content_row, (width, width)), -1),
        axis=1,
        keepdims=True,
    )
    target_col = jnp.max(
        jnp.where(along == down, jnp.broadcast_to(target_row, (width, width)), -1),
        axis=1,
        keepdims=True,
    )
    own_along = share_start + lax.broadcasted_iota(I32, (width, share), 1)
    top_row[...] = jnp.max(jnp.where(target_col == own_along, content_col, -1), axis=0, keepdims=True)
    own_down = share_start + lax.broadcasted_iota(I32, (share, width), 0)
    found = jnp.max(jnp.where(target_row == own_down, content_row, -1), axis=1, keepdims=True)
    top_col[...] = jnp.broadcast_to(found, top_col.shape)
    for half in range(give.shape[0]):
        start = pl.multiple_of((2 * half + place[3]) * share, share)
        give[half] = slab[pl.ds(start, share), :]
    to_scalar.wait()

    def gather(group, carry):
        for slot in range(block):
            local = source_s[0, group * block + slot] - row_start
            owned = (local >= 0) & (local < rows)
            at = jnp.where(owned, local, 0)
            keep = jnp.where(owned, 1.0, 0.0).astype(F32)
            send[group, slot : slot + 1, :] = slab[pl.ds(at, 1), :] * keep
        return carry

    lax.fori_loop(0, groups, gather, 0)


def pack_kernel(moved, got, send):
    groups, block, _ = moved.shape
    part = send.shape[1] - got.shape[1]
    for target in range(groups):
        send[target, :block, :] = moved[target]
    fill = got.shape[1] - block
    for target in range(groups):
        send[target, block : block + fill, :] = got[0, block:, :]
        send[target, block + fill :, :] = got[0, target * part : (target + 1) * part, :]


def plane_sum_kernel(place, got, panel, top_row, send, panel_out, top_panel, *, block):
    groups = got.shape[0]
    first = groups // 2
    part = send.shape[1] - block
    fill = got.shape[1] - block - part
    moved = got[0, :block, :]
    for source in range(1, groups):
        moved = moved + got[source, :block, :]
    top = got[0, block + fill :, :]
    for source in range(1, first):
        top = top + got[source, block + fill :, :]
    for target in range(send.shape[0]):
        send[target, :block, :] = moved
        send[target, block:, :] = top
    for source in range(first):
        top_panel[source * fill : (source + 1) * fill, :] = got[source, block : block + fill, :]
    share = top_row.shape[1]
    width = top_panel.shape[1]
    lands = top_row[...]
    slot = lax.broadcasted_iota(I32, (width, share), 0)
    chosen = jnp.where(slot == lands, 1.0, 0.0).astype(F32)
    replaced = jnp.dot(top_panel[...], chosen, precision=HIGHEST, preferred_element_type=F32)
    own = panel[:, pl.ds(pl.multiple_of(place[2] * share, share), share)]
    panel_out[...] = jnp.where(lands >= 0, replaced, own)


def column_kernel(got, panel, rows_out, panel_out):
    groups, both, _ = got.shape
    block = rows_out.shape[0] // 2
    part = both - block
    moved = got[0, :block, :]
    for source in range(1, groups):
        moved = moved + got[source, :block, :]
    rows_out[:block, :] = moved
    for source in range(groups):
        rows_out[block + source * part : block + (source + 1) * part, :] = got[source, block:, :]
    for target in range(panel_out.shape[0]):
        panel_out[target] = panel[...]


def update_kernel(place, slab, slab_got, panel, rows_in, l_inv, u_inv, top_col, out, *, n_y):
    groups, both, columns = rows_in.shape
    block = both // 2
    part = block // n_y
    width = l_inv.shape[0]
    share = slab.shape[0]
    panel_p = panel[...].reshape(width, share)
    lower = lax.dot_general(
        panel_p, u_inv[...], (((0,), (0,)), ((), ())), precision=HIGHEST, preferred_element_type=F32
    )
    moved = rows_in[:, :block, :].reshape(width, columns)
    top = rows_in[:, block:, :].reshape(width, columns)
    upper = jnp.dot(l_inv[...], moved, precision=HIGHEST, preferred_element_type=F32)
    lands = top_col[:, :1]
    slot = lax.broadcasted_iota(I32, (share, width), 1)
    member, rest = slot // block, slot % block
    holds = (rest // part) * (groups * part) + member * part + rest % part
    chosen = jnp.where(holds == lands, 1.0, 0.0).astype(F32)
    replaced = jnp.dot(chosen, top, precision=HIGHEST, preferred_element_type=F32)
    slab_p = jnp.where(lands >= 0, replaced, slab[...] + slab_got[...])
    out[...] = slab_p - jnp.dot(lower, upper, precision=HIGHEST, preferred_element_type=F32)

    @pl.when(place[1] == 0)
    def _():
        out[:width, :] = upper


def shards(slab_parts, panel_t, l_inv, u_inv, pivots):
    slab_local = slab_parts[0]
    rows, columns = slab_local.shape
    width = l_inv.shape[0]
    tall = panel_t.shape[0]
    n_y, n_z = lax.axis_size("y"), lax.axis_size("z")
    n_depth = lax.axis_size(DEPTH)
    n_plane = lax.axis_size(PLANE)
    share = rows // n_depth
    block = width // n_plane
    part = block // n_y
    fill = tall // n_depth
    row_index = lax.axis_index(ROW)
    layer = lax.axis_index(DEPTH)
    x_index = lax.axis_index("xl")
    core = lax.axis_index("core")
    row_start = row_index * rows
    place = jnp.stack([row_start, row_start + layer * share, layer, 1 - core]).astype(I32)
    swap = [(0, 1), (1, 0)]
    params = pltpu.CompilerParams(vmem_limit_bytes=32 << 20)

    wide = pltpu.CompilerParams(vmem_limit_bytes=56 << 20)

    top = pl.pallas_call(
        functools.partial(top_kernel, layers=n_depth),
        out_shape=jax.ShapeDtypeStruct((n_y, width // n_y + fill, columns), F32),
        in_specs=[ANY, ANY],
        out_specs=VMEM,
        scratch_shapes=[pltpu.SemaphoreType.DMA((2, n_y))],
        compiler_params=wide,
        name="top_rows",
    )(slab_local, panel_t)
    top, place = lax.optimization_barrier((top, place))
    top = lax.all_to_all(top, "y", 0, 0)

    moved, top_row, top_col, give = pl.pallas_call(
        pivot_kernel,
        out_shape=(
            jax.ShapeDtypeStruct((n_plane, block, columns), F32),
            jax.ShapeDtypeStruct((1, share), I32),
            jax.ShapeDtypeStruct((share, 128), I32),
            jax.ShapeDtypeStruct((n_depth // 2, share, columns), F32),
        ),
        in_specs=[SMEM, VMEM, VMEM],
        out_specs=(VMEM, VMEM, VMEM, VMEM),
        scratch_shapes=[
            pltpu.VMEM((8, width), I32),
            pltpu.SMEM((8, width), I32),
            pltpu.SemaphoreType.DMA,
        ],
        compiler_params=params,
        cost_estimate=pl.CostEstimate(
            flops=2 * width * rows * columns, bytes_accessed=16 * rows * columns, transcendentals=0
        ),
        name="pivot_rows",
    )(place, pivots.reshape(1, width), slab_local)

    send = pl.pallas_call(
        pack_kernel,
        out_shape=jax.ShapeDtypeStruct((n_plane, block + fill + part, columns), F32),
        in_specs=[VMEM, VMEM],
        out_specs=VMEM,
        compiler_params=params,
        name="pack_plane",
    )(moved, top)
    send, give = lax.optimization_barrier((send, give))
    core_got = lax.ppermute(give, "core", swap)
    by_core = slab_local.reshape(n_depth // 2, 2, share, columns)
    half = lax.dynamic_index_in_dim(by_core, core, 1, keepdims=False) + core_got
    slab_own = lax.dynamic_index_in_dim(half, x_index, 0, keepdims=False)
    slab_give = lax.dynamic_index_in_dim(half, 1 - x_index, 0, keepdims=False)
    got = lax.all_to_all(send, PLANE, 0, 0)
    send, panel_own = pl.pallas_call(
        functools.partial(plane_sum_kernel, block=block),
        out_shape=(
            jax.ShapeDtypeStruct((n_y, block + part, columns), F32),
            jax.ShapeDtypeStruct((tall, share), F32),
        ),
        in_specs=[SMEM, VMEM, VMEM, VMEM],
        out_specs=(VMEM, VMEM),
        scratch_shapes=[pltpu.VMEM((tall, width), F32)],
        compiler_params=params,
        name="plane_sum",
    )(place, got, panel_t, top_row)
    slab_got = lax.ppermute(slab_give, "xl", swap)
    got = lax.all_to_all(send, "y", 0, 0)
    got, slab_got = lax.optimization_barrier((got, slab_got))
    rows_out, panel_out = pl.pallas_call(
        column_kernel,
        out_shape=(
            jax.ShapeDtypeStruct((2 * block, columns), F32),
            jax.ShapeDtypeStruct((n_z, tall, share), F32),
        ),
        in_specs=[VMEM, VMEM],
        out_specs=(VMEM, VMEM),
        compiler_params=params,
        name="column_sum",
    )(got, panel_own)
    panel_p = lax.all_to_all(panel_out, "z", 0, 0)
    rows_in = lax.all_gather(rows_out, PLANE)
    return pl.pallas_call(
        functools.partial(update_kernel, n_y=n_y),
        out_shape=jax.ShapeDtypeStruct((share, columns), F32),
        in_specs=[SMEM] + [VMEM] * 7,
        out_specs=VMEM,
        compiler_params=params,
        name="update_rows",
    )(place, slab_own, slab_got, panel_p, rows_in, l_inv, u_inv, top_col)


def solution(mesh):
    n_row, n_col, n_depth = mesh.devices.shape
    fine = Mesh(
        mesh.devices.reshape(n_row // 2, 2, n_col, n_depth // 2, 2), ("y", "xh", "z", "xl", "core")
    )
    placed = (P(DEPTH, ROW, "z"), P("z", ROW), P(), P(), P())
    return jax.shard_map(
        shards,
        mesh=fine,
        in_specs=placed,
        out_specs=P(("y", "xh", "xl", "core"), "z"),
        check_vma=False,
    )
```

```python
import functools

import jax
import jax.numpy as jnp
from jax import lax
from jax.experimental import pallas as pl
from jax.experimental.pallas import tpu as pltpu
from jax.sharding import Mesh
from jax.sharding import PartitionSpec as P

ROW = ("y", "xh")
DEPTH = ("xl", "core")
PLANE = ("xh", "xl", "core")
HIGHEST = lax.Precision.HIGHEST
F32 = jnp.float32
I32 = jnp.int32
ANY = pl.BlockSpec(memory_space=pl.ANY)
VMEM = pl.BlockSpec(memory_space=pltpu.VMEM)
SMEM = pl.BlockSpec(memory_space=pltpu.SMEM)


def lane_lookup(table, index):
    width = table.shape[1]
    parts = []
    for at in range(0, width, 128):
        wanted = index[:, at : at + 128]
        found = jnp.zeros_like(wanted)
        for start in range(0, width, 128):
            chunk = table[:, start : start + 128]
            taken = jnp.take_along_axis(chunk, wanted & 127, axis=1)
            found = jnp.where((wanted >= start) & (wanted < start + 128), taken, found)
        parts.append(found)
    return jnp.concatenate(parts, axis=1)


def top_kernel(slab, panel, send, sems, *, layers):
    groups, both, _ = send.shape
    fill = panel.shape[0] // layers
    block = both - fill
    width = groups * block
    start = pl.multiple_of(lax.axis_index(DEPTH) * fill, fill)
    copies = []
    for target in range(groups):
        rows = slab.at[pl.ds(target * block, block), :]
        part = panel.at[pl.ds(start, fill), pl.ds(0, width)]
        copies.append(pltpu.make_async_copy(rows, send.at[target, pl.ds(0, block)], sems.at[0, target]))
        copies.append(pltpu.make_async_copy(part, send.at[target, pl.ds(block, fill)], sems.at[1, target]))
    for copy in copies:
        copy.start()
    for copy in copies:
        copy.wait()


def pivot_kernel(place, pivots, slab, send, top_row, top_col, first, second, source_v, source_s, sem):
    rows, columns = slab.shape
    width = pivots.shape[1]
    groups, block, _ = send.shape
    share = top_row.shape[1]
    row_start = place[0]
    share_start = place[1]
    along = lax.broadcasted_iota(I32, (width, width), 1)
    down = lax.broadcasted_iota(I32, (width, width), 0)
    pivot_row = pivots[...]
    pivot_all = jnp.broadcast_to(pivot_row, (width, width))
    pivot_col = jnp.max(jnp.where(along == down, pivot_all, -1), axis=1, keepdims=True)
    earlier = down < along
    same = pivot_col == pivot_all
    before = jnp.max(jnp.where((pivot_col == along) & earlier, down, -1), axis=0, keepdims=True)
    last = jnp.max(jnp.where(same & earlier, down, -1), axis=0, keepdims=True)
    later = jnp.max(jnp.where(same & (down > along), 1, 0), axis=0, keepdims=True)
    slots = lax.broadcasted_iota(I32, (8, width), 1)
    before = jnp.broadcast_to(before, (8, width))
    content = jnp.where(before < 0, slots, before)
    span = 1
    while span < width:
        content = lane_lookup(content, content)
        span *= 2
    last = jnp.broadcast_to(last, (8, width))
    source = jnp.where(
        last < 0,
        jnp.broadcast_to(pivot_row, (8, width)),
        lane_lookup(content, jnp.maximum(last, 0)),
    )
    source_v[...] = source
    to_scalar = pltpu.make_async_copy(source_v, source_s, sem)
    to_scalar.start()
    content_row = content[:1]
    target_row = jnp.where((later == 0) & (pivot_row >= width), pivot_row, -1)
    content_col = jnp.max(
        jnp.where(along == down, jnp.broadcast_to(content_row, (width, width)), -1),
        axis=1,
        keepdims=True,
    )
    target_col = jnp.max(
        jnp.where(along == down, jnp.broadcast_to(target_row, (width, width)), -1),
        axis=1,
        keepdims=True,
    )
    own_along = share_start + lax.broadcasted_iota(I32, (width, share), 1)
    top_row[...] = jnp.max(jnp.where(target_col == own_along, content_col, -1), axis=0, keepdims=True)
    square = lax.broadcasted_iota(I32, (128, 128), 0) == lax.broadcasted_iota(I32, (128, 128), 1)
    for start in range(0, share, 128):
        piece = jnp.broadcast_to(top_row[:, start : start + 128], (128, 128))
        found = jnp.max(jnp.where(square, piece, -1), axis=1, keepdims=True)
        top_col[start : start + 128, :] = jnp.broadcast_to(found, (128, 128))
    local_row = source[:1] - row_start
    owned_row = jnp.where((local_row >= 0) & (local_row < rows), 1.0, 0.0).astype(F32)
    owned_all = jnp.broadcast_to(owned_row, (width, width))
    owned = jnp.max(jnp.where(along == down, owned_all, 0.0), axis=1, keepdims=True)
    for half, give in enumerate((first, second)):
        start = pl.multiple_of((2 * half + place[3]) * share, share)
        give[...] = slab[pl.ds(start, share), :]
    to_scalar.wait()

    def gather(group, carry):
        for slot in range(block):
            at = jnp.clip(source_s[0, group * block + slot] - row_start, 0, rows - 1)
            send[group, slot : slot + 1, :] = slab[pl.ds(at, 1), :]
        return carry

    lax.fori_loop(0, groups, gather, 0)
    for group in range(groups):
        keep = owned[group * block : (group + 1) * block] > 0.0
        send[group] = jnp.where(keep, send[group], 0.0)


def pack_kernel(moved, got, send):
    groups, block, _ = moved.shape
    part = send.shape[1] - got.shape[1]
    for target in range(groups):
        send[target, :block, :] = moved[target]
    fill = got.shape[1] - block
    for target in range(groups):
        send[target, block : block + fill, :] = got[0, block:, :]
        send[target, block + fill :, :] = got[0, target * part : (target + 1) * part, :]


def plane_sum_kernel(got, send, *, block):
    groups = got.shape[0]
    part = send.shape[1] - block
    both = got.shape[1]
    moved = got[0, :block, :]
    for source in range(1, groups):
        moved = moved + got[source, :block, :]
    top = got[0, both - part :, :]
    for source in range(1, groups // 2):
        top = top + got[source, both - part :, :]
    for target in range(send.shape[0]):
        send[target, :block, :] = moved
        send[target, block:, :] = top


def panel_kernel(place, got, panel, top_row, panel_out, top_panel, *, block):
    layers = got.shape[0] // 2
    fill = panel.shape[0] // layers
    for source in range(layers):
        top_panel[source * fill : (source + 1) * fill, :] = got[source, block : block + fill, :]
    share = top_row.shape[1]
    width = top_panel.shape[1]
    lands = top_row[...]
    slot = lax.broadcasted_iota(I32, (width, share), 0)
    chosen = jnp.where(slot == lands, 1.0, 0.0).astype(F32)
    replaced = jnp.dot(top_panel[...], chosen, precision=HIGHEST, preferred_element_type=F32)
    own = panel[:, pl.ds(pl.multiple_of(place[2] * share, share), share)]
    fixed = jnp.where(lands >= 0, replaced, own)
    for target in range(panel_out.shape[0]):
        panel_out[target] = fixed


def column_kernel(got, rows_out):
    groups, both, _ = got.shape
    block = rows_out.shape[0] // 2
    part = both - block
    moved = got[0, :block, :]
    for source in range(1, groups):
        moved = moved + got[source, :block, :]
    rows_out[:block, :] = moved
    for source in range(groups):
        rows_out[block + source * part : block + (source + 1) * part, :] = got[source, block:, :]


def update_kernel(place, slab, slab_got, panel, rows_in, l_inv, u_inv, top_col, out, *, n_y):
    groups, both, columns = rows_in.shape
    block = both // 2
    part = block // n_y
    width = l_inv.shape[0]
    share = slab.shape[0]
    panel_p = panel[...].reshape(width, share)
    lower = lax.dot_general(
        panel_p, u_inv[...], (((0,), (0,)), ((), ())), precision=HIGHEST, preferred_element_type=F32
    )
    moved = rows_in[:, :block, :].reshape(width, columns)
    top = rows_in[:, block:, :].reshape(width, columns)
    upper = jnp.dot(l_inv[...], moved, precision=HIGHEST, preferred_element_type=F32)
    lands = top_col[:, :1]
    slot = lax.broadcasted_iota(I32, (share, width), 1)
    member, rest = slot // block, slot % block
    holds = (rest // part) * (groups * part) + member * part + rest % part
    chosen = jnp.where(holds == lands, 1.0, 0.0).astype(F32)
    replaced = jnp.dot(chosen, top, precision=HIGHEST, preferred_element_type=F32)
    slab_p = jnp.where(lands >= 0, replaced, slab[...] + slab_got[...])
    out[...] = slab_p - jnp.dot(lower, upper, precision=HIGHEST, preferred_element_type=F32)

    @pl.when(place[1] == 0)
    def _():
        out[:width, :] = upper


def shards(slab_parts, panel_t, l_inv, u_inv, pivots):
    slab_local = slab_parts[0]
    rows, columns = slab_local.shape
    width = l_inv.shape[0]
    tall = panel_t.shape[0]
    n_y, n_z = lax.axis_size("y"), lax.axis_size("z")
    n_depth = lax.axis_size(DEPTH)
    n_plane = lax.axis_size(PLANE)
    share = rows // n_depth
    block = width // n_plane
    part = block // n_y
    fill = tall // n_depth
    row_index = lax.axis_index(ROW)
    layer = lax.axis_index(DEPTH)
    x_index = lax.axis_index("xl")
    core = lax.axis_index("core")
    row_start = row_index * rows
    place = jnp.stack([row_start, row_start + layer * share, layer, 1 - core]).astype(I32)
    swap = [(0, 1), (1, 0)]
    params = pltpu.CompilerParams(vmem_limit_bytes=32 << 20)

    wide = pltpu.CompilerParams(vmem_limit_bytes=56 << 20)

    top = pl.pallas_call(
        functools.partial(top_kernel, layers=n_depth),
        out_shape=jax.ShapeDtypeStruct((n_y, width // n_y + fill, columns), F32),
        in_specs=[ANY, ANY],
        out_specs=VMEM,
        scratch_shapes=[pltpu.SemaphoreType.DMA((2, n_y))],
        compiler_params=wide,
        name="top_rows",
    )(slab_local, panel_t)
    top, place = lax.optimization_barrier((top, place))
    top = lax.all_to_all(top, "y", 0, 0)

    moved, top_row, top_col, first, second = pl.pallas_call(
        pivot_kernel,
        out_shape=(
            jax.ShapeDtypeStruct((n_plane, block, columns), F32),
            jax.ShapeDtypeStruct((1, share), I32),
            jax.ShapeDtypeStruct((share, 128), I32),
            jax.ShapeDtypeStruct((share, columns), F32),
            jax.ShapeDtypeStruct((share, columns), F32),
        ),
        in_specs=[SMEM, VMEM, VMEM],
        out_specs=(VMEM,) * 5,
        scratch_shapes=[
            pltpu.VMEM((8, width), I32),
            pltpu.SMEM((8, width), I32),
            pltpu.SemaphoreType.DMA,
        ],
        compiler_params=params,
        cost_estimate=pl.CostEstimate(
            flops=2 * width * rows * columns, bytes_accessed=16 * rows * columns, transcendentals=0
        ),
        name="pivot_rows",
    )(place, pivots.reshape(1, width), slab_local)

    send = pl.pallas_call(
        pack_kernel,
        out_shape=jax.ShapeDtypeStruct((n_plane, block + fill + part, columns), F32),
        in_specs=[VMEM, VMEM],
        out_specs=VMEM,
        compiler_params=params,
        name="pack_plane",
    )(moved, top)
    first_got = lax.ppermute(first, "core", swap)
    second_got = lax.ppermute(second, "core", swap)
    near = lax.dynamic_slice_in_dim(slab_local, (2 * x_index + core) * share, share)
    far = lax.dynamic_slice_in_dim(slab_local, (2 * (1 - x_index) + core) * share, share)
    slab_own = near + jnp.where(x_index == 0, first_got, second_got)
    slab_give = far + jnp.where(x_index == 0, second_got, first_got)
    got = lax.all_to_all(send, PLANE, 0, 0)
    send = pl.pallas_call(
        functools.partial(plane_sum_kernel, block=block),
        out_shape=jax.ShapeDtypeStruct((n_y, block + part, columns), F32),
        in_specs=[VMEM],
        out_specs=VMEM,
        compiler_params=params,
        name="plane_sum",
    )(got)
    panel_out = pl.pallas_call(
        functools.partial(panel_kernel, block=block),
        out_shape=jax.ShapeDtypeStruct((n_z, tall, share), F32),
        in_specs=[SMEM, VMEM, VMEM, VMEM],
        out_specs=VMEM,
        scratch_shapes=[pltpu.VMEM((tall, width), F32)],
        compiler_params=params,
        cost_estimate=pl.CostEstimate(
            flops=2 * rows * width * columns, bytes_accessed=8 * rows * columns, transcendentals=0
        ),
        name="panel_columns",
    )(place, got, panel_t, top_row)
    slab_got = lax.ppermute(slab_give, "xl", swap)
    got = lax.all_to_all(send, "y", 0, 0)
    got, panel_out, slab_got = lax.optimization_barrier((got, panel_out, slab_got))
    panel_p = lax.all_to_all(panel_out, "z", 0, 0)
    rows_out = pl.pallas_call(
        column_kernel,
        out_shape=jax.ShapeDtypeStruct((2 * block, columns), F32),
        in_specs=[VMEM],
        out_specs=VMEM,
        compiler_params=params,
        name="column_sum",
    )(got)
    rows_in = lax.all_gather(rows_out, PLANE)
    return pl.pallas_call(
        functools.partial(update_kernel, n_y=n_y),
        out_shape=jax.ShapeDtypeStruct((share, columns), F32),
        in_specs=[SMEM] + [VMEM] * 7,
        out_specs=VMEM,
        compiler_params=params,
        name="update_rows",
    )(place, slab_own, slab_got, panel_p, rows_in, l_inv, u_inv, top_col)


def solution(mesh):
    n_row, n_col, n_depth = mesh.devices.shape
    fine = Mesh(
        mesh.devices.reshape(n_row // 2, 2, n_col, n_depth // 2, 2), ("y", "xh", "z", "xl", "core")
    )
    placed = (P(DEPTH, ROW, "z"), P("z", ROW), P(), P(), P())
    return jax.shard_map(
        shards,
        mesh=fine,
        in_specs=placed,
        out_specs=P(("y", "xh", "xl", "core"), "z"),
        check_vma=False,
    )
```

```python
import functools

import jax
import jax.numpy as jnp
from jax import lax
from jax.experimental import pallas as pl
from jax.experimental.pallas import tpu as pltpu
from jax.sharding import Mesh
from jax.sharding import PartitionSpec as P

ROW = ("y", "xh")
DEPTH = ("xl", "core")
PLANE = ("xh", "xl", "core")
HIGHEST = lax.Precision.HIGHEST
F32 = jnp.float32
I32 = jnp.int32
ANY = pl.BlockSpec(memory_space=pl.ANY)
VMEM = pl.BlockSpec(memory_space=pltpu.VMEM)
SMEM = pl.BlockSpec(memory_space=pltpu.SMEM)


def lane_lookup(table, index):
    width = table.shape[1]
    parts = []
    for at in range(0, width, 128):
        wanted = index[:, at : at + 128]
        found = jnp.zeros_like(wanted)
        for start in range(0, width, 128):
            chunk = table[:, start : start + 128]
            taken = jnp.take_along_axis(chunk, wanted & 127, axis=1)
            found = jnp.where((wanted >= start) & (wanted < start + 128), taken, found)
        parts.append(found)
    return jnp.concatenate(parts, axis=1)


def top_kernel(slab, panel, send, sems, *, layers):
    groups, both, _ = send.shape
    fill = panel.shape[0] // layers
    block = both - fill
    width = groups * block
    start = pl.multiple_of(lax.axis_index(DEPTH) * fill, fill)
    copies = []
    for target in range(groups):
        rows = slab.at[pl.ds(target * block, block), :]
        part = panel.at[pl.ds(start, fill), pl.ds(0, width)]
        copies.append(pltpu.make_async_copy(rows, send.at[target, pl.ds(0, block)], sems.at[0, target]))
        copies.append(pltpu.make_async_copy(part, send.at[target, pl.ds(block, fill)], sems.at[1, target]))
    for copy in copies:
        copy.start()
    for copy in copies:
        copy.wait()


def pivot_kernel(place, pivots, slab, send, top_row, top_col, first, second, source_v, source_s, sems):
    rows, columns = slab.shape
    width = pivots.shape[1]
    groups, block, _ = send.shape
    share = top_row.shape[1]
    row_start = place[0]
    share_start = place[1]
    gives = []
    for half, give in enumerate((first, second)):
        start = pl.multiple_of((2 * half + place[3]) * share, share)
        gives.append(pltpu.make_async_copy(slab.at[pl.ds(start, share)], give, sems.at[1 + half]))
        gives[-1].start()
    along = lax.broadcasted_iota(I32, (width, width), 1)
    down = lax.broadcasted_iota(I32, (width, width), 0)
    pivot_row = pivots[...]
    pivot_all = jnp.broadcast_to(pivot_row, (width, width))
    pivot_col = jnp.max(jnp.where(along == down, pivot_all, -1), axis=1, keepdims=True)
    earlier = down < along
    same = pivot_col == pivot_all
    before = jnp.max(jnp.where((pivot_col == along) & earlier, down, -1), axis=0, keepdims=True)
    last = jnp.max(jnp.where(same & earlier, down, -1), axis=0, keepdims=True)
    later = jnp.max(jnp.where(same & (down > along), 1, 0), axis=0, keepdims=True)
    slots = lax.broadcasted_iota(I32, (8, width), 1)
    before = jnp.broadcast_to(before, (8, width))
    content = jnp.where(before < 0, slots, before)
    span = 1
    while span < width:
        content = lane_lookup(content, content)
        span *= 2
    last = jnp.broadcast_to(last, (8, width))
    source = jnp.where(
        last < 0,
        jnp.broadcast_to(pivot_row, (8, width)),
        lane_lookup(content, jnp.maximum(last, 0)),
    )
    source_v[...] = source
    to_scalar = pltpu.make_async_copy(source_v, source_s, sems.at[0])
    to_scalar.start()
    content_row = content[:1]
    target_row = jnp.where((later == 0) & (pivot_row >= width), pivot_row, -1)
    content_col = jnp.max(
        jnp.where(along == down, jnp.broadcast_to(content_row, (width, width)), -1),
        axis=1,
        keepdims=True,
    )
    target_col = jnp.max(
        jnp.where(along == down, jnp.broadcast_to(target_row, (width, width)), -1),
        axis=1,
        keepdims=True,
    )
    own_along = share_start + lax.broadcasted_iota(I32, (width, share), 1)
    top_row[...] = jnp.max(jnp.where(target_col == own_along, content_col, -1), axis=0, keepdims=True)
    square = lax.broadcasted_iota(I32, (128, 128), 0) == lax.broadcasted_iota(I32, (128, 128), 1)
    for start in range(0, share, 128):
        piece = jnp.broadcast_to(top_row[:, start : start + 128], (128, 128))
        found = jnp.max(jnp.where(square, piece, -1), axis=1, keepdims=True)
        top_col[start : start + 128, :] = jnp.broadcast_to(found, (128, 128))
    local_row = source[:1] - row_start
    owned_row = jnp.where((local_row >= 0) & (local_row < rows), 1.0, 0.0).astype(F32)
    owned_all = jnp.broadcast_to(owned_row, (width, width))
    owned = jnp.max(jnp.where(along == down, owned_all, 0.0), axis=1, keepdims=True)
    to_scalar.wait()

    def gather(group, carry):
        for slot in range(block):
            at = jnp.clip(source_s[0, group * block + slot] - row_start, 0, rows - 1)
            send[group, slot : slot + 1, :] = slab[pl.ds(at, 1), :]
        return carry

    lax.fori_loop(0, groups, gather, 0)
    for group in range(groups):
        keep = owned[group * block : (group + 1) * block] > 0.0
        send[group] = jnp.where(keep, send[group], 0.0)
    for copy in gives:
        copy.wait()


def pack_kernel(moved, got, send):
    groups, block, _ = moved.shape
    part = send.shape[1] - got.shape[1]
    for target in range(groups):
        send[target, :block, :] = moved[target]
    fill = got.shape[1] - block
    for target in range(groups):
        send[target, block : block + fill, :] = got[0, block:, :]
        send[target, block + fill :, :] = got[0, target * part : (target + 1) * part, :]


def plane_sum_kernel(got, send, *, block):
    groups = got.shape[0]
    part = send.shape[1] - block
    both = got.shape[1]
    moved = got[0, :block, :]
    for source in range(1, groups):
        moved = moved + got[source, :block, :]
    top = got[0, both - part :, :]
    for source in range(1, groups // 2):
        top = top + got[source, both - part :, :]
    for target in range(send.shape[0]):
        send[target, :block, :] = moved
        send[target, block:, :] = top


def panel_kernel(place, got, panel, top_row, panel_out, top_panel, *, block):
    layers = got.shape[0] // 2
    fill = panel.shape[0] // layers
    for source in range(layers):
        top_panel[source * fill : (source + 1) * fill, :] = got[source, block : block + fill, :]
    share = top_row.shape[1]
    width = top_panel.shape[1]
    lands = top_row[...]
    slot = lax.broadcasted_iota(I32, (width, share), 0)
    chosen = jnp.where(slot == lands, 1.0, 0.0).astype(F32)
    replaced = jnp.dot(top_panel[...], chosen, precision=HIGHEST, preferred_element_type=F32)
    own = panel[:, pl.ds(pl.multiple_of(place[2] * share, share), share)]
    fixed = jnp.where(lands >= 0, replaced, own)
    for target in range(panel_out.shape[0]):
        panel_out[target] = fixed


def column_kernel(got, rows_out):
    groups, both, _ = got.shape
    block = rows_out.shape[0] // 2
    part = both - block
    moved = got[0, :block, :]
    for source in range(1, groups):
        moved = moved + got[source, :block, :]
    rows_out[:block, :] = moved
    for source in range(groups):
        rows_out[block + source * part : block + (source + 1) * part, :] = got[source, block:, :]


def update_kernel(place, slab, slab_got, panel, rows_in, l_inv, u_inv, top_col, out, *, n_y):
    groups, both, columns = rows_in.shape
    block = both // 2
    part = block // n_y
    width = l_inv.shape[0]
    share = slab.shape[0]
    panel_p = panel[...].reshape(width, share)
    lower = lax.dot_general(
        panel_p, u_inv[...], (((0,), (0,)), ((), ())), precision=HIGHEST, preferred_element_type=F32
    )
    moved = rows_in[:, :block, :].reshape(width, columns)
    top = rows_in[:, block:, :].reshape(width, columns)
    upper = jnp.dot(l_inv[...], moved, precision=HIGHEST, preferred_element_type=F32)
    lands = top_col[:, :1]
    slot = lax.broadcasted_iota(I32, (share, width), 1)
    member, rest = slot // block, slot % block
    holds = (rest // part) * (groups * part) + member * part + rest % part
    chosen = jnp.where(holds == lands, 1.0, 0.0).astype(F32)
    replaced = jnp.dot(chosen, top, precision=HIGHEST, preferred_element_type=F32)
    slab_p = jnp.where(lands >= 0, replaced, slab[...] + slab_got[...])
    out[...] = slab_p - jnp.dot(lower, upper, precision=HIGHEST, preferred_element_type=F32)

    @pl.when(place[1] == 0)
    def _():
        out[:width, :] = upper


def shards(slab_parts, panel_t, l_inv, u_inv, pivots):
    slab_local = slab_parts[0]
    rows, columns = slab_local.shape
    width = l_inv.shape[0]
    tall = panel_t.shape[0]
    n_y, n_z = lax.axis_size("y"), lax.axis_size("z")
    n_depth = lax.axis_size(DEPTH)
    n_plane = lax.axis_size(PLANE)
    share = rows // n_depth
    block = width // n_plane
    part = block // n_y
    fill = tall // n_depth
    row_index = lax.axis_index(ROW)
    layer = lax.axis_index(DEPTH)
    x_index = lax.axis_index("xl")
    core = lax.axis_index("core")
    row_start = row_index * rows
    place = jnp.stack([row_start, row_start + layer * share, layer, 1 - core]).astype(I32)
    swap = [(0, 1), (1, 0)]
    params = pltpu.CompilerParams(vmem_limit_bytes=32 << 20)

    wide = pltpu.CompilerParams(vmem_limit_bytes=56 << 20)

    top = pl.pallas_call(
        functools.partial(top_kernel, layers=n_depth),
        out_shape=jax.ShapeDtypeStruct((n_y, width // n_y + fill, columns), F32),
        in_specs=[ANY, ANY],
        out_specs=VMEM,
        scratch_shapes=[pltpu.SemaphoreType.DMA((2, n_y))],
        compiler_params=wide,
        name="top_rows",
    )(slab_local, panel_t)
    top, place = lax.optimization_barrier((top, place))
    top = lax.all_to_all(top, "y", 0, 0)

    moved, top_row, top_col, first, second = pl.pallas_call(
        pivot_kernel,
        out_shape=(
            jax.ShapeDtypeStruct((n_plane, block, columns), F32),
            jax.ShapeDtypeStruct((1, share), I32),
            jax.ShapeDtypeStruct((share, 128), I32),
            jax.ShapeDtypeStruct((share, columns), F32),
            jax.ShapeDtypeStruct((share, columns), F32),
        ),
        in_specs=[SMEM, VMEM, VMEM],
        out_specs=(VMEM, VMEM, VMEM, ANY, ANY),
        scratch_shapes=[
            pltpu.VMEM((8, width), I32),
            pltpu.SMEM((8, width), I32),
            pltpu.SemaphoreType.DMA((3,)),
        ],
        compiler_params=params,
        cost_estimate=pl.CostEstimate(
            flops=2 * width * rows * columns, bytes_accessed=16 * rows * columns, transcendentals=0
        ),
        name="pivot_rows",
    )(place, pivots.reshape(1, width), slab_local)

    send = pl.pallas_call(
        pack_kernel,
        out_shape=jax.ShapeDtypeStruct((n_plane, block + fill + part, columns), F32),
        in_specs=[VMEM, VMEM],
        out_specs=VMEM,
        compiler_params=params,
        name="pack_plane",
    )(moved, top)
    first_got = lax.ppermute(first, "core", swap)
    second_got = lax.ppermute(second, "core", swap)
    near = lax.dynamic_slice_in_dim(slab_local, (2 * x_index + core) * share, share)
    far = lax.dynamic_slice_in_dim(slab_local, (2 * (1 - x_index) + core) * share, share)
    slab_own = near + jnp.where(x_index == 0, first_got, second_got)
    slab_give = far + jnp.where(x_index == 0, second_got, first_got)
    got = lax.all_to_all(send, PLANE, 0, 0)
    send = pl.pallas_call(
        functools.partial(plane_sum_kernel, block=block),
        out_shape=jax.ShapeDtypeStruct((n_y, block + part, columns), F32),
        in_specs=[VMEM],
        out_specs=VMEM,
        compiler_params=params,
        name="plane_sum",
    )(got)
    panel_out = pl.pallas_call(
        functools.partial(panel_kernel, block=block),
        out_shape=jax.ShapeDtypeStruct((n_z, tall, share), F32),
        in_specs=[SMEM, VMEM, VMEM, VMEM],
        out_specs=VMEM,
        scratch_shapes=[pltpu.VMEM((tall, width), F32)],
        compiler_params=params,
        cost_estimate=pl.CostEstimate(
            flops=2 * rows * width * columns, bytes_accessed=8 * rows * columns, transcendentals=0
        ),
        name="panel_columns",
    )(place, got, panel_t, top_row)
    slab_got = lax.ppermute(slab_give, "xl", swap)
    got = lax.all_to_all(send, "y", 0, 0)
    got, panel_out, slab_got = lax.optimization_barrier((got, panel_out, slab_got))
    panel_p = lax.all_to_all(panel_out, "z", 0, 0)
    rows_out = pl.pallas_call(
        column_kernel,
        out_shape=jax.ShapeDtypeStruct((2 * block, columns), F32),
        in_specs=[VMEM],
        out_specs=VMEM,
        compiler_params=params,
        name="column_sum",
    )(got)
    rows_in = lax.all_gather(rows_out, PLANE)
    return pl.pallas_call(
        functools.partial(update_kernel, n_y=n_y),
        out_shape=jax.ShapeDtypeStruct((share, columns), F32),
        in_specs=[SMEM] + [VMEM] * 7,
        out_specs=VMEM,
        compiler_params=params,
        name="update_rows",
    )(place, slab_own, slab_got, panel_p, rows_in, l_inv, u_inv, top_col)


def solution(mesh):
    n_row, n_col, n_depth = mesh.devices.shape
    fine = Mesh(
        mesh.devices.reshape(n_row // 2, 2, n_col, n_depth // 2, 2), ("y", "xh", "z", "xl", "core")
    )
    placed = (P(DEPTH, ROW, "z"), P("z", ROW), P(), P(), P())
    return jax.shard_map(
        shards,
        mesh=fine,
        in_specs=placed,
        out_specs=P(("y", "xh", "xl", "core"), "z"),
        check_vma=False,
    )
```

```python
import functools

import jax
import jax.numpy as jnp
from jax import lax
from jax.experimental import pallas as pl
from jax.experimental.pallas import tpu as pltpu
from jax.sharding import Mesh
from jax.sharding import PartitionSpec as P

ROW = ("y", "xh")
DEPTH = ("xl", "core")
PLANE = ("xh", "xl", "core")
HIGHEST = lax.Precision.HIGHEST
F32 = jnp.float32
I32 = jnp.int32
ANY = pl.BlockSpec(memory_space=pl.ANY)
VMEM = pl.BlockSpec(memory_space=pltpu.VMEM)
SMEM = pl.BlockSpec(memory_space=pltpu.SMEM)


def lane_lookup(table, index):
    width = table.shape[1]
    parts = []
    for at in range(0, width, 128):
        wanted = index[:, at : at + 128]
        found = jnp.zeros_like(wanted)
        for start in range(0, width, 128):
            chunk = table[:, start : start + 128]
            taken = jnp.take_along_axis(chunk, wanted & 127, axis=1)
            found = jnp.where((wanted >= start) & (wanted < start + 128), taken, found)
        parts.append(found)
    return jnp.concatenate(parts, axis=1)


def top_kernel(slab, panel, send, staged, sems, *, layers):
    groups, both, _ = send.shape
    fill = panel.shape[0] // layers
    block = both - fill
    width = groups * block
    start = pl.multiple_of(lax.axis_index(DEPTH) * fill, fill)
    arrivals, departures = [], []
    for target in range(groups):
        rows = slab.at[pl.ds(target * block, block), :]
        part = panel.at[pl.ds(start, fill), pl.ds(0, width)]
        here = staged.at[target]
        arrivals.append(pltpu.make_async_copy(rows, here.at[pl.ds(0, block)], sems.at[0, target]))
        arrivals.append(pltpu.make_async_copy(part, here.at[pl.ds(block, fill)], sems.at[1, target]))
        departures.append(pltpu.make_async_copy(here, send.at[target], sems.at[2, target]))
    for copy in arrivals:
        copy.start()
    for target in range(groups):
        arrivals[2 * target].wait()
        arrivals[2 * target + 1].wait()
        departures[target].start()
    for copy in departures:
        copy.wait()


def pivot_kernel(place, pivots, slab, send, top_row, top_col, first, second, source_v, source_s, sems):
    rows, columns = slab.shape
    width = pivots.shape[1]
    groups, block, _ = send.shape
    share = top_row.shape[1]
    row_start = place[0]
    share_start = place[1]
    gives = []
    for half, give in enumerate((first, second)):
        start = pl.multiple_of((2 * half + place[3]) * share, share)
        gives.append(pltpu.make_async_copy(slab.at[pl.ds(start, share)], give, sems.at[1 + half]))
        gives[-1].start()
    along = lax.broadcasted_iota(I32, (width, width), 1)
    down = lax.broadcasted_iota(I32, (width, width), 0)
    pivot_row = pivots[...]
    pivot_all = jnp.broadcast_to(pivot_row, (width, width))
    pivot_col = jnp.max(jnp.where(along == down, pivot_all, -1), axis=1, keepdims=True)
    earlier = down < along
    same = pivot_col == pivot_all
    before = jnp.max(jnp.where((pivot_col == along) & earlier, down, -1), axis=0, keepdims=True)
    last = jnp.max(jnp.where(same & earlier, down, -1), axis=0, keepdims=True)
    later = jnp.max(jnp.where(same & (down > along), 1, 0), axis=0, keepdims=True)
    slots = lax.broadcasted_iota(I32, (8, width), 1)
    before = jnp.broadcast_to(before, (8, width))
    content = jnp.where(before < 0, slots, before)
    span = 1
    while span < width:
        content = lane_lookup(content, content)
        span *= 2
    last = jnp.broadcast_to(last, (8, width))
    source = jnp.where(
        last < 0,
        jnp.broadcast_to(pivot_row, (8, width)),
        lane_lookup(content, jnp.maximum(last, 0)),
    )
    source_v[...] = source
    to_scalar = pltpu.make_async_copy(source_v, source_s, sems.at[0])
    to_scalar.start()
    content_row = content[:1]
    target_row = jnp.where((later == 0) & (pivot_row >= width), pivot_row, -1)
    content_col = jnp.max(
        jnp.where(along == down, jnp.broadcast_to(content_row, (width, width)), -1),
        axis=1,
        keepdims=True,
    )
    target_col = jnp.max(
        jnp.where(along == down, jnp.broadcast_to(target_row, (width, width)), -1),
        axis=1,
        keepdims=True,
    )
    own_along = share_start + lax.broadcasted_iota(I32, (width, share), 1)
    top_row[...] = jnp.max(jnp.where(target_col == own_along, content_col, -1), axis=0, keepdims=True)
    square = lax.broadcasted_iota(I32, (128, 128), 0) == lax.broadcasted_iota(I32, (128, 128), 1)
    for start in range(0, share, 128):
        piece = jnp.broadcast_to(top_row[:, start : start + 128], (128, 128))
        found = jnp.max(jnp.where(square, piece, -1), axis=1, keepdims=True)
        top_col[start : start + 128, :] = jnp.broadcast_to(found, (128, 128))
    local_row = source[:1] - row_start
    owned_row = jnp.where((local_row >= 0) & (local_row < rows), 1.0, 0.0).astype(F32)
    owned_all = jnp.broadcast_to(owned_row, (width, width))
    owned = jnp.max(jnp.where(along == down, owned_all, 0.0), axis=1, keepdims=True)
    to_scalar.wait()

    def gather(group, carry):
        for slot in range(block):
            at = jnp.clip(source_s[0, group * block + slot] - row_start, 0, rows - 1)
            send[group, slot : slot + 1, :] = slab[pl.ds(at, 1), :]
        return carry

    lax.fori_loop(0, groups, gather, 0)
    for group in range(groups):
        keep = owned[group * block : (group + 1) * block] > 0.0
        send[group] = jnp.where(keep, send[group], 0.0)
    for copy in gives:
        copy.wait()


def pack_kernel(moved, got, send):
    groups, block, _ = moved.shape
    part = send.shape[1] - got.shape[1]
    for target in range(groups):
        send[target, :block, :] = moved[target]
    fill = got.shape[1] - block
    for target in range(groups):
        send[target, block : block + fill, :] = got[0, block:, :]
        send[target, block + fill :, :] = got[0, target * part : (target + 1) * part, :]


def plane_sum_kernel(got, send, *, block):
    groups = got.shape[0]
    part = send.shape[1] - block
    both = got.shape[1]
    moved = got[0, :block, :]
    for source in range(1, groups):
        moved = moved + got[source, :block, :]
    top = got[0, both - part :, :]
    for source in range(1, groups // 2):
        top = top + got[source, both - part :, :]
    for target in range(send.shape[0]):
        send[target, :block, :] = moved
        send[target, block:, :] = top


def panel_kernel(place, got, panel, top_row, panel_out, top_panel, *, block):
    layers = got.shape[0] // 2
    fill = panel.shape[0] // layers
    for source in range(layers):
        top_panel[source * fill : (source + 1) * fill, :] = got[source, block : block + fill, :]
    share = top_row.shape[1]
    width = top_panel.shape[1]
    lands = top_row[...]
    slot = lax.broadcasted_iota(I32, (width, share), 0)
    chosen = jnp.where(slot == lands, 1.0, 0.0).astype(F32)
    replaced = jnp.dot(top_panel[...], chosen, precision=HIGHEST, preferred_element_type=F32)
    own = panel[:, pl.ds(pl.multiple_of(place[2] * share, share), share)]
    fixed = jnp.where(lands >= 0, replaced, own)
    for target in range(panel_out.shape[0]):
        panel_out[target] = fixed


def column_kernel(got, rows_out):
    groups, both, _ = got.shape
    block = rows_out.shape[0] // 2
    part = both - block
    moved = got[0, :block, :]
    for source in range(1, groups):
        moved = moved + got[source, :block, :]
    rows_out[:block, :] = moved
    for source in range(groups):
        rows_out[block + source * part : block + (source + 1) * part, :] = got[source, block:, :]


def update_kernel(place, slab, slab_got, panel, rows_in, l_inv, u_inv, top_col, out, *, n_y):
    groups, both, columns = rows_in.shape
    block = both // 2
    part = block // n_y
    width = l_inv.shape[0]
    share = slab.shape[0]
    panel_p = panel[...].reshape(width, share)
    lower = lax.dot_general(
        panel_p, u_inv[...], (((0,), (0,)), ((), ())), precision=HIGHEST, preferred_element_type=F32
    )
    moved = rows_in[:, :block, :].reshape(width, columns)
    top = rows_in[:, block:, :].reshape(width, columns)
    upper = jnp.dot(l_inv[...], moved, precision=HIGHEST, preferred_element_type=F32)
    lands = top_col[:, :1]
    slot = lax.broadcasted_iota(I32, (share, width), 1)
    member, rest = slot // block, slot % block
    holds = (rest // part) * (groups * part) + member * part + rest % part
    chosen = jnp.where(holds == lands, 1.0, 0.0).astype(F32)
    replaced = jnp.dot(chosen, top, precision=HIGHEST, preferred_element_type=F32)
    slab_p = jnp.where(lands >= 0, replaced, slab[...] + slab_got[...])
    out[...] = slab_p - jnp.dot(lower, upper, precision=HIGHEST, preferred_element_type=F32)

    @pl.when(place[1] == 0)
    def _():
        out[:width, :] = upper


def shards(slab_parts, panel_t, l_inv, u_inv, pivots):
    slab_local = slab_parts[0]
    rows, columns = slab_local.shape
    width = l_inv.shape[0]
    tall = panel_t.shape[0]
    n_y, n_z = lax.axis_size("y"), lax.axis_size("z")
    n_depth = lax.axis_size(DEPTH)
    n_plane = lax.axis_size(PLANE)
    share = rows // n_depth
    block = width // n_plane
    part = block // n_y
    fill = tall // n_depth
    row_index = lax.axis_index(ROW)
    layer = lax.axis_index(DEPTH)
    x_index = lax.axis_index("xl")
    core = lax.axis_index("core")
    row_start = row_index * rows
    place = jnp.stack([row_start, row_start + layer * share, layer, 1 - core]).astype(I32)
    swap = [(0, 1), (1, 0)]
    params = pltpu.CompilerParams(vmem_limit_bytes=32 << 20)

    wide = pltpu.CompilerParams(vmem_limit_bytes=56 << 20)

    top = pl.pallas_call(
        functools.partial(top_kernel, layers=n_depth),
        out_shape=jax.ShapeDtypeStruct((n_y, width // n_y + fill, columns), F32),
        in_specs=[ANY, ANY],
        out_specs=ANY,
        scratch_shapes=[
            pltpu.VMEM((n_y, width // n_y + fill, columns), F32),
            pltpu.SemaphoreType.DMA((3, n_y)),
        ],
        compiler_params=wide,
        name="top_rows",
    )(slab_local, panel_t)
    top, place = lax.optimization_barrier((top, place))
    top = lax.all_to_all(top, "y", 0, 0)

    moved, top_row, top_col, first, second = pl.pallas_call(
        pivot_kernel,
        out_shape=(
            jax.ShapeDtypeStruct((n_plane, block, columns), F32),
            jax.ShapeDtypeStruct((1, share), I32),
            jax.ShapeDtypeStruct((share, 128), I32),
            jax.ShapeDtypeStruct((share, columns), F32),
            jax.ShapeDtypeStruct((share, columns), F32),
        ),
        in_specs=[SMEM, VMEM, VMEM],
        out_specs=(VMEM, VMEM, VMEM, ANY, ANY),
        scratch_shapes=[
            pltpu.VMEM((8, width), I32),
            pltpu.SMEM((8, width), I32),
            pltpu.SemaphoreType.DMA((3,)),
        ],
        compiler_params=params,
        cost_estimate=pl.CostEstimate(
            flops=2 * width * rows * columns, bytes_accessed=16 * rows * columns, transcendentals=0
        ),
        name="pivot_rows",
    )(place, pivots.reshape(1, width), slab_local)

    send = pl.pallas_call(
        pack_kernel,
        out_shape=jax.ShapeDtypeStruct((n_plane, block + fill + part, columns), F32),
        in_specs=[VMEM, VMEM],
        out_specs=VMEM,
        compiler_params=params,
        name="pack_plane",
    )(moved, top)
    first_got = lax.ppermute(first, "core", swap)
    second_got = lax.ppermute(second, "core", swap)
    near = lax.dynamic_slice_in_dim(slab_local, (2 * x_index + core) * share, share)
    far = lax.dynamic_slice_in_dim(slab_local, (2 * (1 - x_index) + core) * share, share)
    slab_own = near + jnp.where(x_index == 0, first_got, second_got)
    slab_give = far + jnp.where(x_index == 0, second_got, first_got)
    got = lax.all_to_all(send, PLANE, 0, 0)
    send = pl.pallas_call(
        functools.partial(plane_sum_kernel, block=block),
        out_shape=jax.ShapeDtypeStruct((n_y, block + part, columns), F32),
        in_specs=[VMEM],
        out_specs=VMEM,
        compiler_params=params,
        name="plane_sum",
    )(got)
    panel_out = pl.pallas_call(
        functools.partial(panel_kernel, block=block),
        out_shape=jax.ShapeDtypeStruct((n_z, tall, share), F32),
        in_specs=[SMEM, VMEM, VMEM, VMEM],
        out_specs=VMEM,
        scratch_shapes=[pltpu.VMEM((tall, width), F32)],
        compiler_params=params,
        cost_estimate=pl.CostEstimate(
            flops=2 * rows * width * columns, bytes_accessed=8 * rows * columns, transcendentals=0
        ),
        name="panel_columns",
    )(place, got, panel_t, top_row)
    slab_got = lax.ppermute(slab_give, "xl", swap)
    got = lax.all_to_all(send, "y", 0, 0)
    got, panel_out, slab_got = lax.optimization_barrier((got, panel_out, slab_got))
    panel_p = lax.all_to_all(panel_out, "z", 0, 0)
    rows_out = pl.pallas_call(
        column_kernel,
        out_shape=jax.ShapeDtypeStruct((2 * block, columns), F32),
        in_specs=[VMEM],
        out_specs=VMEM,
        compiler_params=params,
        name="column_sum",
    )(got)
    rows_in = lax.all_gather(rows_out, PLANE)
    return pl.pallas_call(
        functools.partial(update_kernel, n_y=n_y),
        out_shape=jax.ShapeDtypeStruct((share, columns), F32),
        in_specs=[SMEM] + [VMEM] * 7,
        out_specs=VMEM,
        compiler_params=params,
        name="update_rows",
    )(place, slab_own, slab_got, panel_p, rows_in, l_inv, u_inv, top_col)


def solution(mesh):
    n_row, n_col, n_depth = mesh.devices.shape
    fine = Mesh(
        mesh.devices.reshape(n_row // 2, 2, n_col, n_depth // 2, 2), ("y", "xh", "z", "xl", "core")
    )
    placed = (P(DEPTH, ROW, "z"), P("z", ROW), P(), P(), P())
    return jax.shard_map(
        shards,
        mesh=fine,
        in_specs=placed,
        out_specs=P(("y", "xh", "xl", "core"), "z"),
        check_vma=False,
    )
```
